256 devices in a mesh: grp: 4 (over x_lo, core), blk: 64 (over z, y, x_hi).
Axes of the slice: x: 4 (x_hi: 2, x_lo: 2; x = x_hi * 2 + x_lo), y: 4, z: 8, core: 2. Of those that a mesh axis runs over, the one named last changes fastest.
Arguments:
- mem_keys: bfloat16 [1048576, 128], P(('grp', 'blk'))
- mem_values: bfloat16 [1048576, 512], P(('grp', 'blk'))
- offsets: int32 [4, 64], P('grp', 'blk'), may hold values from 0 to 2048, as said below
- block_skip: int32 [4, 64], P('grp', 'blk'), may hold values from 0 to 63, as said below
- queries: bfloat16 [65536, 128], P('blk')
Outputs:
- retrieved: bfloat16 [65536, 512], P('blk', 'grp')
The draws below stay inside these ranges and needn't reach their ends.
Inputs may be any that keep to these rules, and one draw needn't show every extreme that they name: `offsets`: each window lies inside its device's resident rows. block_skip[g, j] names one of the blocks that attend to slab (g, j), and every query block is named by fewer than all of the slabs it attends to.
All inputs are finite; a program needn't handle non-finite values.
Results may differ from the reference program's by a relative error of at most 0.0048.
Values may be sent and summed in bfloat16 or wider, within the bound.
A program may use at most 192 MiB of HBM per device.

```python
import jax
import jax.numpy as jnp
from jax import lax

DK = 128
DV = 512
QB = 1024
SLAB = 2048
STEPS = 4
RES = 4096
NG = 4
NB = 64
MEM = 1048576
NQ = 65536


def shared_keys(key):
    return jnp.clip(jax.random.normal(key, (MEM, DK), jnp.float32), -5.0, 5.0)


def draw_mem_keys(key, part):
    base = shared_keys(key)
    keys = 0.5 * base
    return keys.astype(jnp.bfloat16)


def draw_mem_values(key, part):
    key = jax.random.fold_in(key, 17)
    values = 0.2 * jnp.clip(jax.random.normal(key, (MEM, DV), jnp.float32), -5.0, 5.0)
    return values.astype(jnp.bfloat16)


def draw_queries(key, part):
    key = jax.random.fold_in(key, 7)
    values = jnp.clip(jax.random.normal(key, (NQ, DK), jnp.float32), -4.0, 4.0) * 1.5
    return values.astype(jnp.bfloat16)


def draw_offsets(key, part):
    key = jax.random.fold_in(key, 9)
    starts = jax.random.randint(key, (NG, NB), 0, SLAB + 1, jnp.int32)
    return starts.at[0, 0].set(0).at[0, 1].set(SLAB)


def draw_block_skip(key, part):
    key = jax.random.fold_in(key, 13)
    back = jax.random.randint(key, (NG, NB), 0, STEPS, jnp.int32)
    back = back.at[0, 0].set(1).at[1, 0].set(0)
    column = jnp.arange(NB, dtype=jnp.int32)[None, :]
    return ((column - back) % NB).astype(jnp.int32)


def setup_inputs(seed: int = 0) -> dict:
    splits = jax.random.split(jax.random.key(seed), 6)
    mem_keys = draw_mem_keys(jax.random.fold_in(splits[5], 71), 0)
    mem_values = draw_mem_values(jax.random.fold_in(splits[5], 71), 0)
    offsets = draw_offsets(jax.random.fold_in(splits[5], 71), 0)
    block_skip = draw_block_skip(jax.random.fold_in(splits[5], 71), 0)
    queries = draw_queries(jax.random.fold_in(splits[5], 71), 0)
    return dict(mem_keys=mem_keys, mem_values=mem_values, offsets=offsets, block_skip=block_skip, queries=queries)


lowest = -1e+30

def slab_partial(block, keys_w, vals_w, scale):
    scores = lax.dot_general(block, keys_w, (((1,), (1,)), ((), ())), preferred_element_type=jnp.float32) * scale
    top = lax.optimization_barrier(jnp.max(scores, axis=1))
    prob = jnp.exp(scores - top[:, None])
    total = lax.optimization_barrier(jnp.sum(prob, axis=1))
    acc = jnp.dot(prob.astype(jnp.bfloat16), vals_w, preferred_element_type=jnp.float32)
    return (top, total, acc)

def join(first, second):
    top = jnp.maximum(first[0], second[0])
    fa = jnp.exp(first[0] - top)
    fb = jnp.exp(second[0] - top)
    return (top, first[1] * fa + second[1] * fb, first[2] * fa[..., None] + second[2] * fb[..., None])

def reference(mem_keys, mem_values, offsets, block_skip, queries):
    scale = DK ** (-0.5)

    def one_block(index):
        block = lax.dynamic_slice_in_dim(queries, index * QB, QB, 0)
        state = (jnp.full((QB,), lowest, jnp.float32), jnp.zeros((QB,), jnp.float32), jnp.zeros((QB, DV), jnp.float32))
        for group in range(NG):
            for step in range(STEPS):
                column = ((index + step) % NB).astype(jnp.int32)
                device = (group * NB + column).astype(jnp.int32)
                start = (device * RES + offsets[group, column]).astype(jnp.int32)
                keys_w = lax.dynamic_slice_in_dim(mem_keys, start, SLAB, 0)
                vals_w = lax.dynamic_slice_in_dim(mem_values, start, SLAB, 0)
                top, total, acc = slab_partial(block, keys_w, vals_w, scale)
                keep = block_skip[group, column] != index
                top = jnp.where(keep, top, lowest)
                total = jnp.where(keep, total, 0.0)
                acc = jnp.where(keep, acc, 0.0)
                state = join(state, (top, total, acc))
        ratio = state[2] / state[1][:, None]
        mean_sq = lax.optimization_barrier(jnp.mean(ratio * ratio, axis=1))
        return (ratio * lax.rsqrt(mean_sq + 1e-06)[:, None]).astype(jnp.bfloat16)
    outs = lax.map(one_block, jnp.arange(NB, dtype=jnp.int32))
    return outs.reshape(NB * QB, DV)
```

```python
import functools

import jax
import jax.numpy as jnp
from jax import lax
from jax.experimental import pallas as pl
from jax.experimental.pallas import tpu as pltpu
from jax.sharding import PartitionSpec as P

MESH = pl.DeviceIdType.MESH
LOG2E = 1.4426950408889634
LOWEST = -1e30
HIGHEST = 3e38
TILES = 4
STEPS = 4
VISITS = TILES * STEPS
PAIR_LAG = 3
ITERS = 23


def joined(a, ms_a, b, ms_b):
    ma, la = ms_a[0:1, :], ms_a[1:2, :]
    mb, lb = ms_b[0:1, :], ms_b[1:2, :]
    top = jnp.maximum(ma, mb)
    fa = jnp.exp2(ma - top)
    fb = jnp.exp2(mb - top)
    total = la * fa + lb * fb
    return [x * fa + y.astype(jnp.float32) * fb for x, y in zip(a, b)], top, total


def kernel(
    skip_ref, k_ref, v_ref, q_ref, out_ref,
    vt, qs, own, own_ms, keep, keep_ms, hold, hold_ms, home, home_ms, ratio,
    cs, cs_ms, cr, cr_ms, ps, ps_ms, pr, pr_ms,
    xs, xs_ms, xr, xr_ms, ys, ys_ms, yr, yr_ms, ss, sr,
    q_send, q_recv, f_send, f_recv,
    send_sem, c_recv, p_recv, x_recv, y_recv, s_recv,
):
    g = lax.axis_index("grp")
    j = lax.axis_index("blk")
    nb = lax.axis_size("blk")
    core = lax.rem(g, 2)
    xl = lax.div(g, 2)
    xh = lax.rem(j, 2)
    g_core = g + 1 - 2 * core
    g_pair = lax.rem(g + 2, 4)
    g_both = g_core + 2 - 4 * xl

    def at(d):
        return lax.rem(j + nb + d, nb)

    cross = (g_pair, at(1 - 2 * xh))
    down = (g, at(-2))
    rows = q_ref.shape[0]
    tq = rows // TILES
    half = rows // 2
    width = v_ref.shape[1]
    scale = q_ref.shape[1] ** (-0.5) * LOG2E

    barrier = pltpu.get_barrier_semaphore()
    partners = [
        (g_core, j), (g_pair, j), (g_both, j), (g, at(2)), (g, at(-2)),
        (g_pair, at(1)), (g_pair, at(-1)), (g_pair, at(3)), (g_pair, at(-3)),
    ]
    for partner in partners:
        pl.semaphore_signal(barrier, inc=1, device_id=partner, device_id_type=MESH)
    pl.semaphore_wait(barrier, len(partners))

    def remote(src, dst, send, recv, device):
        return pltpu.make_async_remote_copy(
            src_ref=src, dst_ref=dst, send_sem=send, recv_sem=recv,
            device_id=device, device_id_type=MESH,
        )

    mine = pl.ds(core * half, half)
    theirs = pl.ds((1 - core) * half, half)

    def q_copy(step, device):
        return remote(
            q_ref.at[mine], qs.at[step, mine], q_send.at[step], q_recv.at[step], device
        )

    def q_forward(step):
        return remote(
            qs.at[step, mine], qs.at[step, mine], f_send.at[step], f_recv.at[step], (g_core, j)
        )

    q_out = [None, q_copy(1, (g, at(2))), q_copy(2, (g_pair, at(3))), q_copy(3, (g_pair, at(1)))]
    q_out[1].start()
    q_out[2].start()
    q_out[3].start()

    qs[0] = q_ref[...]
    for q in range(4):
        spot = 2 * lax.rem(core + q % 2, 2) + q // 2
        vt[spot] = v_ref[:, q * 128 : (q + 1) * 128].T

    def two(data_src, ms_src, data_dst, ms_dst, sem, recv, device):
        remote(data_src, data_dst, send_sem.at[2 * sem], recv.at[0], device).start()
        remote(ms_src, ms_dst, send_sem.at[2 * sem + 1], recv.at[1], device).start()

    def arrived(data, ms, recv):
        pltpu.make_async_copy(data, data, recv.at[0]).wait()
        pltpu.make_async_copy(ms, ms, recv.at[1]).wait()

    def send_cross(res, top, total, slot):
        xs[slot] = res.astype(jnp.bfloat16)
        xs_ms[slot, 0:1, :] = top
        xs_ms[slot, 1:2, :] = total
        two(xs.at[slot], xs_ms.at[slot], xr.at[slot], xr_ms.at[slot], 2, x_recv.at[slot], cross)

    def send_down(res, top, total, slot):
        ys[slot] = res.astype(jnp.bfloat16)
        ys_ms[slot, 0:1, :] = top
        ys_ms[slot, 1:2, :] = total
        two(ys.at[slot], ys_ms.at[slot], yr.at[slot], yr_ms.at[slot], 3, y_recv.at[slot], down)

    def compute(n):
        step = lax.div(n, TILES)
        tile = lax.rem(n, TILES)
        shift = jnp.where(step == 0, 0, jnp.where(step == 1, 2, jnp.where(step == 2, 3, 1)))
        block = lax.rem(j + nb - shift, nb)
        kept = skip_ref[0, 0] != block
        q = qs[step, pl.ds(pl.multiple_of(tile * tq, tq), tq), :]
        s = lax.dot_general(
            k_ref[...], q, (((1,), (1,)), ((), ())), preferred_element_type=jnp.float32
        )
        top = jnp.max(s, axis=0, keepdims=True)
        ref = jnp.where(kept, top, HIGHEST)
        p = jnp.exp2((s - ref) * scale)
        total = jnp.sum(p, axis=0, keepdims=True)
        acc = jnp.dot(
            vt[...].reshape(width, vt.shape[2]), p.astype(jnp.bfloat16),
            preferred_element_type=jnp.float32,
        )
        own[n, 0] = acc[0:128]
        own[n, 1] = acc[128:256]
        cs[n, 0] = acc[256:384].astype(jnp.bfloat16)
        cs[n, 1] = acc[384:512].astype(jnp.bfloat16)
        cs_ms[n, 0:1, :] = jnp.where(kept, top * scale, LOWEST)
        cs_ms[n, 1:2, :] = total
        two(cs.at[n], cs_ms.at[n], cr.at[n], cr_ms.at[n], 0, c_recv.at[n], (g_core, j))

    def core_merge(n):
        kx = jnp.where(n < 2 * TILES, xl, 1 - xl)
        arrived(cr.at[n], cr_ms.at[n], c_recv.at[n])
        both = ([own[n, kx], own[n, 1 - kx]], [cr[n, kx], cr[n, 1 - kx]])
        (stay, go), top, total = joined(both[0], cs_ms[n], both[1], cr_ms[n])
        keep[n] = stay
        ps[n] = go.astype(jnp.bfloat16)
        ps_ms[n, 0:1, :] = top
        ps_ms[n, 1:2, :] = total
        two(ps.at[n], ps_ms.at[n], pr.at[n], pr_ms.at[n], 1, p_recv.at[n], (g_pair, j))

    def pair_merge(n):
        step = lax.div(n, TILES)
        tile = lax.rem(n, TILES)
        arrived(pr.at[n], pr_ms.at[n], p_recv.at[n])
        (res,), top, total = joined([keep[n]], ps_ms[n], [pr[n]], pr_ms[n])

        @pl.when(step == 0)
        def _():
            home[tile] = res
            home_ms[tile, 0:1, :] = top
            home_ms[tile, 1:2, :] = total

        @pl.when(step == 1)
        def _():
            hold[tile] = res
            hold_ms[tile, 0:1, :] = top
            hold_ms[tile, 1:2, :] = total

        @pl.when(jnp.logical_and(step == 2, xh == 0))
        def _():
            send_down(res, top, total, 4 + tile)

        @pl.when(jnp.logical_and(step == 2, xh == 1))
        def _():
            send_cross(res, top, total, tile)

        @pl.when(jnp.logical_and(step == 3, xh == 0))
        def _():
            slot = 4 + tile
            arrived(yr.at[slot], yr_ms.at[slot], y_recv.at[slot])
            keep[n] = res
            keep_ms[0:1, :] = top
            keep_ms[1:2, :] = total
            (res2,), top2, total2 = joined([keep[n]], keep_ms, [yr[slot]], yr_ms[slot])
            send_cross(res2, top2, total2, tile)

        @pl.when(jnp.logical_and(step == 3, xh == 1))
        def _():
            send_cross(res, top, total, 4 + tile)

    def late_merge(tile):
        arrived(xr.at[tile], xr_ms.at[tile], x_recv.at[tile])
        (res,), top, total = joined([hold[tile]], hold_ms[tile], [xr[tile]], xr_ms[tile])
        send_down(res, top, total, tile)

    def finish(tile, extra):
        arrived(yr.at[tile], yr_ms.at[tile], y_recv.at[tile])
        if extra:
            slot = 4 + tile
            arrived(xr.at[slot], xr_ms.at[slot], x_recv.at[slot])
            (res,), top, total = joined([home[tile]], home_ms[tile], [xr[slot]], xr_ms[slot])
            home[tile] = res
            home_ms[tile, 0:1, :] = top
            home_ms[tile, 1:2, :] = total
        (res,), top, total = joined([home[tile]], home_ms[tile], [yr[tile]], yr_ms[tile])
        r = res / total
        ratio[tile] = r
        ss[tile] = jnp.broadcast_to(jnp.sum(r * r, axis=0, keepdims=True), ss.shape[1:])
        for d, partner in enumerate((g_core, g_pair, g_both)):
            remote(
                ss.at[tile], sr.at[d, tile], send_sem.at[8 + d], s_recv.at[d, tile], (partner, j)
            ).start()

    def iteration(n, _):
        for step in range(1, STEPS):
            @pl.when(n == TILES * step)
            def _():
                pltpu.make_async_copy(
                    qs.at[step, theirs], qs.at[step, theirs], f_recv.at[step]
                ).wait()

        @pl.when(n < VISITS)
        def _():
            compute(n)

        @pl.when(jnp.logical_and(n >= 1, n < VISITS + 1))
        def _():
            core_merge(n - 1)

        @pl.when(jnp.logical_and(n >= PAIR_LAG, n < VISITS + PAIR_LAG))
        def _():
            pair_merge(n - PAIR_LAG)

        late = 13 + 4 * xh

        @pl.when(jnp.logical_and(n >= late, n < late + TILES))
        def _():
            late_merge(n - late)

        @pl.when(jnp.logical_and(xh == 0, jnp.logical_and(n >= 17, n < 17 + TILES)))
        def _():
            finish(n - 17, True)

        @pl.when(jnp.logical_and(xh == 1, jnp.logical_and(n >= 19, n < 19 + TILES)))
        def _():
            finish(n - 19, False)

        for step in range(1, STEPS):
            @pl.when(n == TILES * step - 2)
            def _():
                pltpu.make_async_copy(
                    qs.at[step, mine], qs.at[step, mine], q_recv.at[step]
                ).wait()
                q_forward(step).start()

        return 0

    lax.fori_loop(0, ITERS, iteration, 0)

    for tile in range(TILES):
        squares = ss[tile, 0:1, :]
        for d in range(3):
            pltpu.make_async_copy(sr.at[d, tile], sr.at[d, tile], s_recv.at[d, tile]).wait()
        squares = (squares + sr[0, tile, 0:1, :]) + (sr[1, tile, 0:1, :] + sr[2, tile, 0:1, :])
        o = ratio[tile] * lax.rsqrt(squares / width + 1e-06)
        out_ref[pl.ds(tile * tq, tq), :] = o.T.astype(jnp.bfloat16)

    def drained(ref, sem):
        pltpu.make_async_copy(ref, ref, send_sem.at[sem]).wait()

    drained(cs, 0)
    drained(cs_ms, 1)
    drained(ps, 2)
    drained(ps_ms, 3)

    @pl.when(xh == 0)
    def _():
        drained(xs.at[pl.ds(0, 4)], 4)
        drained(xs_ms.at[pl.ds(0, 4)], 5)
        drained(ys, 6)
        drained(ys_ms, 7)

    @pl.when(xh == 1)
    def _():
        drained(xs, 4)
        drained(xs_ms, 5)
        drained(ys.at[pl.ds(0, 4)], 6)
        drained(ys_ms.at[pl.ds(0, 4)], 7)

    for d in range(3):
        drained(ss, 8 + d)
    for step in range(1, STEPS):
        q_out[step].wait_send()
        q_forward(step).wait_send()


def attend(skip, keys, vals, queries):
    rows, dk = queries.shape
    window, width = vals.shape
    tq = rows // TILES
    f32, bf16 = jnp.float32, jnp.bfloat16
    vmem = pltpu.VMEM
    dma = pltpu.SemaphoreType.DMA
    share = width // 4

    def both(n, dtype, *lead):
        return [vmem((n, *lead, share, tq), dtype), vmem((n, 2, tq), f32)]

    scratch = [
        vmem((4, share, window), bf16),
        vmem((STEPS, rows, dk), bf16),
        *both(VISITS, f32, 2),
        vmem((VISITS, share, tq), f32),
        vmem((2, tq), f32),
        *both(TILES, f32),
        *both(TILES, f32),
        vmem((TILES, share, tq), f32),
        *both(VISITS, bf16, 2),
        *both(VISITS, bf16, 2),
        *both(VISITS, bf16),
        *both(VISITS, bf16),
        *both(8, bf16),
        *both(8, bf16),
        *both(8, bf16),
        *both(8, bf16),
        vmem((TILES, 8, tq), f32),
        vmem((3, TILES, 8, tq), f32),
        dma((STEPS,)), dma((STEPS,)), dma((STEPS,)), dma((STEPS,)),
        dma((11,)),
        dma((VISITS, 2)), dma((VISITS, 2)), dma((8, 2)), dma((8, 2)), dma((3, TILES)),
    ]
    return pl.pallas_call(
        kernel,
        out_shape=jax.ShapeDtypeStruct((rows, share), bf16),
        in_specs=[
            pl.BlockSpec(memory_space=pltpu.SMEM),
            pl.BlockSpec(memory_space=vmem),
            pl.BlockSpec(memory_space=vmem),
            pl.BlockSpec(memory_space=vmem),
        ],
        out_specs=pl.BlockSpec(memory_space=vmem),
        scratch_shapes=scratch,
        compiler_params=pltpu.CompilerParams(
            collective_id=0, has_side_effects=True, vmem_limit_bytes=56 * 2**20
        ),
    )(skip, keys, vals, queries)


def body(mem_keys, mem_values, offsets, block_skip, queries):
    window = mem_keys.shape[0] // 2
    start = offsets[0, 0]
    keys_w = lax.dynamic_slice_in_dim(mem_keys, start, window, 0)
    vals_w = lax.dynamic_slice_in_dim(mem_values, start, window, 0)
    return attend(block_skip, keys_w, vals_w, queries)


def solution(mesh):
    placed = (
        P(("grp", "blk"), None),
        P(("grp", "blk"), None),
        P("grp", "blk"),
        P("grp", "blk"),
        P("blk", None),
    )
    return jax.shard_map(
        body, mesh=mesh, in_specs=placed, out_specs=P("blk", "grp"), check_vma=False
    )
```

```python
import jax
import jax.numpy as jnp
from jax import lax
from jax.experimental import pallas as pl
from jax.experimental.pallas import tpu as pltpu
from jax.sharding import PartitionSpec as P

MESH = pl.DeviceIdType.MESH
LOG2E = 1.4426950408889634
LOWEST = -1e30
HIGHEST = 3e38
TILES = 4
STEPS = 4
VISITS = TILES * STEPS
CHUNKS = 8
HEAD = 3
EARLY = 3
Q_LAG = 3
Q_AHEAD = 4
CORE_LAG = 1
PAIR_LAG = 4
HOP_LAG = 3


def joined(parts):
    tops = [ms[0:1, :] for _, ms in parts]
    top = tops[0]
    for other in tops[1:]:
        top = jnp.maximum(top, other)
    total = None
    sums = None
    for (values, ms), own_top in zip(parts, tops):
        f = jnp.exp2(own_top - top)
        mass = ms[1:2, :] * f
        terms = [v.astype(jnp.float32) * f for v in values]
        total = mass if total is None else total + mass
        sums = terms if sums is None else [a + b for a, b in zip(sums, terms)]
    return sums, top, total


def kernel(
    skip_hbm, start_hbm, k_hbm, v_hbm, q_hbm, out_ref,
    skip_ref, start_ref, k_all, v_all, kw, vt, qs, s_even, s_odd, m_even, m_odd,
    own, keep, home, home_ms, ratio,
    cs, cs_ms, cr, cr_ms, ps, ps_ms, pr, pr_ms,
    es, es_ms, er, er_ms, ds, ds_ms, dr, dr_ms, ss, sr,
    load_sem, q_send, q_recv, f_send, f_recv,
    send_sem, c_recv, p_recv, e_recv, d_recv, s_recv,
):
    g = lax.axis_index("grp")
    j = lax.axis_index("blk")
    nb = lax.axis_size("blk")
    core = lax.rem(g, 2)
    xl = lax.div(g, 2)
    g_core = g + 1 - 2 * core
    g_pair = lax.rem(g + 2, 4)
    g_both = g_core + 2 - 4 * xl

    def at(d):
        return lax.rem(j + nb + d, nb)

    rows = q_hbm.shape[0]
    tq = rows // TILES
    half = tq // 2
    window = kw.shape[0]
    width = v_all.shape[1]
    share = width // 4
    scale = q_hbm.shape[1] ** (-0.5) * LOG2E

    loads = [
        pltpu.make_async_copy(src, dst, load_sem.at[i])
        for i, (src, dst) in enumerate(
            ((start_hbm, start_ref), (skip_hbm, skip_ref), (q_hbm, qs.at[0]), (k_hbm, k_all), (v_hbm, v_all))
        )
    ]
    for load in loads:
        load.start()

    barrier = pltpu.get_barrier_semaphore()
    partners = [
        (g_core, j), (g_pair, j), (g_both, j), (g, at(2)), (g, at(-2)),
        (g_pair, at(1)), (g_pair, at(-1)), (g_pair, at(3)), (g_pair, at(-3)),
    ]
    for partner in partners:
        pl.semaphore_signal(barrier, inc=1, device_id=partner, device_id_type=MESH)

    def remote(src, dst, send, recv, device):
        return pltpu.make_async_remote_copy(
            src_ref=src, dst_ref=dst, send_sem=send, recv_sem=recv,
            device_id=device, device_id_type=MESH,
        )

    homes = {1: (g_pair, at(1)), 2: (g, at(2)), 3: (g_pair, at(3))}

    def q_rows(tile, part):
        return pl.ds(tile * tq + part * half, half)

    def q_copy(back, tile):
        return remote(
            qs.at[0, q_rows(tile, core)], qs.at[back, q_rows(tile, core)],
            q_send.at[back], q_recv.at[back, tile], homes[back],
        )

    def q_forward(back, tile):
        piece = qs.at[back, q_rows(tile, core)]
        pltpu.make_async_copy(piece, piece, q_recv.at[back, tile]).wait()
        remote(piece, piece, f_send.at[back], f_recv.at[back, tile], (g_core, j)).start()

    def q_wait(back, tile):
        piece = qs.at[back, q_rows(tile, 1 - core)]
        pltpu.make_async_copy(piece, piece, f_recv.at[back, tile]).wait()

    for load in loads[:4]:
        load.wait()
    start = start_ref[0, 0]

    def windowed(ref, begin, size):
        low = ref[begin : begin + size, :].astype(jnp.float32)
        high = ref[window + begin : window + begin + size, :].astype(jnp.float32)
        row = begin + lax.broadcasted_iota(jnp.int32, low.shape, 0)
        return jnp.where(row >= start, low, high).astype(jnp.bfloat16)

    piece_rows = window // 8
    for c in range(8):
        kw[c * piece_rows : (c + 1) * piece_rows, :] = windowed(k_all, c * piece_rows, piece_rows)
    loads[4].wait()
    for c in range(8):
        piece = windowed(v_all, c * piece_rows, piece_rows)
        for q in range(4):
            spot = 2 * lax.rem(core + q % 2, 2) + q // 2
            vt[spot, :, c * piece_rows : (c + 1) * piece_rows] = piece[
                :, q * share : (q + 1) * share
            ].T

    def two(data_src, ms_src, data_dst, ms_dst, sem, recv, device):
        remote(data_src, data_dst, send_sem.at[2 * sem], recv.at[0], device).start()
        remote(ms_src, ms_dst, send_sem.at[2 * sem + 1], recv.at[1], device).start()

    def arrived(data, ms, recv):
        pltpu.make_async_copy(data, data, recv.at[0]).wait()
        pltpu.make_async_copy(ms, ms, recv.at[1]).wait()

    def visit(n):
        m = n - HEAD
        phase = lax.div(m + 4, 4) - 1
        remote_visit = jnp.logical_and(m >= 0, m < 12)
        back = jnp.where(phase == 2, 1, phase + 2)
        back = jnp.where(remote_visit, back, 0)
        tile = jnp.where(remote_visit, m - 4 * phase, jnp.where(m < 0, n, n - 12))
        return back, tile

    def scores(n, s_ref, c, chunk, q):
        part = slice(c * chunk, (c + 1) * chunk)
        s = lax.dot_general(
            kw[part, :], q, (((1,), (1,)), ((), ())), preferred_element_type=jnp.float32
        )
        s_ref[part, :] = s
        return jnp.max(s, axis=0, keepdims=True)

    def queries_of(n):
        back, tile = visit(n)
        return qs[back, pl.ds(pl.multiple_of(tile * tq, tq), tq), :]

    chunk = window // CHUNKS

    def compute(n, s_now, m_now, s_next, m_next):
        back, _ = visit(n)
        kept = skip_ref[0, 0] != lax.rem(j + nb - back, nb)
        q = queries_of(jnp.minimum(n + 1, VISITS - 1))
        top = m_now[0:1, :]
        ref = jnp.where(kept, top, HIGHEST)
        high = total = None
        probs = []
        for c in range(CHUNKS):
            part = slice(c * chunk, (c + 1) * chunk)
            peak = scores(n, s_next, c, chunk, q)
            high = peak if high is None else jnp.maximum(high, peak)
            p = jnp.exp2((s_now[part, :] - ref) * scale)
            mass = jnp.sum(p, axis=0, keepdims=True)
            total = mass if total is None else total + mass
            probs.append(p.astype(jnp.bfloat16))
        m_next[0:1, :] = high
        acc = jnp.dot(
            vt[...].reshape(width, window), jnp.concatenate(probs, axis=0),
            preferred_element_type=jnp.float32,
        )
        own[n, 0] = acc[0:share]
        own[n, 1] = acc[share : 2 * share]
        cs[n, 0] = acc[2 * share : 3 * share].astype(jnp.bfloat16)
        cs[n, 1] = acc[3 * share : 4 * share].astype(jnp.bfloat16)
        cs_ms[n, 0:1, :] = jnp.where(kept, top * scale, LOWEST)
        cs_ms[n, 1:2, :] = total
        two(cs.at[n], cs_ms.at[n], cr.at[n], cr_ms.at[n], 0, c_recv.at[n], (g_core, j))

    def core_merge(n):
        back, tile = visit(n)
        kx = jnp.where(lax.rem(back, 2) == 0, xl, 1 - xl)
        late = tile >= EARLY
        slot = jnp.maximum(tile - EARLY, 0)
        arrived(cr.at[n], cr_ms.at[n], c_recv.at[n])

        def chip(a, b):
            return [
                ([own[n, a], own[n, b]], cs_ms[n]),
                ([cr[n, a], cr[n, b]], cr_ms[n]),
            ]

        def to_pair(parts):
            (stay, go), top, total = joined(parts)
            keep[n] = stay
            ps[n] = go.astype(jnp.bfloat16)
            ps_ms[n, 0:1, :] = top
            ps_ms[n, 1:2, :] = total
            two(ps.at[n], ps_ms.at[n], pr.at[n], pr_ms.at[n], 1, p_recv.at[n], (g_pair, j))

        @pl.when(jnp.logical_not(jnp.logical_and(late, lax.rem(back, 2) == 0)))
        def _():
            to_pair(chip(kx, 1 - kx))

        @pl.when(jnp.logical_and(late, back == 0))
        def _():
            arrived(er.at[slot], er_ms.at[slot], e_recv.at[slot])
            more = ([er[slot, kx], er[slot, 1 - kx]], er_ms[slot])
            to_pair(chip(kx, 1 - kx) + [more])

        @pl.when(jnp.logical_and(late, back == 2))
        def _():
            (low, high), top, total = joined(chip(0, 1))
            es[slot, 0] = low.astype(jnp.bfloat16)
            es[slot, 1] = high.astype(jnp.bfloat16)
            es_ms[slot, 0:1, :] = top
            es_ms[slot, 1:2, :] = total
            two(
                es.at[slot], es_ms.at[slot], er.at[slot], er_ms.at[slot], 2, e_recv.at[slot],
                (g, at(-2)),
            )

    def pair_merge(n):
        back, tile = visit(n)

        def paired():
            arrived(pr.at[n], pr_ms.at[n], p_recv.at[n])
            (res,), top, total = joined([([keep[n]], ps_ms[n]), ([pr[n]], pr_ms[n])])
            return res, top, total

        @pl.when(back == 0)
        def _():
            res, top, total = paired()
            home[tile] = res
            home_ms[tile, 0:1, :] = top
            home_ms[tile, 1:2, :] = total

        def send_home(b):
            res, top, total = paired()
            ds[b - 1, tile] = res.astype(jnp.bfloat16)
            ds_ms[b - 1, tile, 0:1, :] = top
            ds_ms[b - 1, tile, 1:2, :] = total
            two(
                ds.at[b - 1, tile], ds_ms.at[b - 1, tile], dr.at[b - 1, tile],
                dr_ms.at[b - 1, tile], 2 + b, d_recv.at[b - 1, tile],
                (g if b == 2 else g_pair, at(-b)),
            )

        for b in (1, 3):
            @pl.when(back == b)
            def _():
                send_home(b)

        @pl.when(jnp.logical_and(back == 2, tile < EARLY))
        def _():
            send_home(2)

    def finish(tile):
        def collect(backs):
            for b in backs:
                arrived(dr.at[b - 1, tile], dr_ms.at[b - 1, tile], d_recv.at[b - 1, tile])
            (res,), _, total = joined(
                [([home[tile]], home_ms[tile])]
                + [([dr[b - 1, tile]], dr_ms[b - 1, tile]) for b in backs]
            )
            r = res / total
            ratio[tile] = r
            ss[tile] = jnp.broadcast_to(jnp.sum(r * r, axis=0, keepdims=True), ss.shape[1:])

        @pl.when(tile < EARLY)
        def _():
            collect((1, 2, 3))

        @pl.when(tile >= EARLY)
        def _():
            collect((1, 3))

        for d, partner in enumerate((g_core, g_pair, g_both)):
            remote(
                ss.at[tile], sr.at[d, tile], send_sem.at[12 + d], s_recv.at[d, tile], (partner, j)
            ).start()

    def send_visit(n):
        back, tile = visit(n)
        for b in range(1, STEPS):
            @pl.when(back == b)
            def _():
                q_copy(b, tile).start()

    def forward_visit(n):
        back, tile = visit(n)
        for b in range(1, STEPS):
            @pl.when(back == b)
            def _():
                q_forward(b, tile)

    def wait_visit(n):
        back, tile = visit(n)

        @pl.when(back > 0)
        def _():
            q_wait(back, tile)

    def iteration(n, s_now, m_now, s_next, m_next):
        @pl.when(n < 12 - Q_AHEAD)
        def _():
            send_visit(n + HEAD + Q_AHEAD)

        @pl.when(n < VISITS - 1)
        def _():
            wait_visit(n + 1)

        @pl.when(n < VISITS)
        def _():
            compute(n, s_now, m_now, s_next, m_next)

        @pl.when(n < VISITS - Q_LAG)
        def _():
            forward_visit(n + Q_LAG)

        @pl.when(jnp.logical_and(n >= CORE_LAG, n < VISITS + CORE_LAG))
        def _():
            core_merge(n - CORE_LAG)

        @pl.when(jnp.logical_and(n >= PAIR_LAG, n < VISITS + PAIR_LAG))
        def _():
            pair_merge(n - PAIR_LAG)

        last = HEAD + 8 + PAIR_LAG + HOP_LAG

        @pl.when(jnp.logical_and(n >= last, n < last + TILES))
        def _():
            finish(n - last)

    q0 = queries_of(0)
    high = None
    for c in range(CHUNKS):
        peak = scores(0, s_even, c, chunk, q0)
        high = peak if high is None else jnp.maximum(high, peak)
    m_even[0:1, :] = high

    pl.semaphore_wait(barrier, len(partners))
    for tile in range(Q_AHEAD):
        q_copy(2, tile).start()

    def two_iterations(u, _):
        iteration(2 * u, s_even, m_even, s_odd, m_odd)
        iteration(2 * u + 1, s_odd, m_odd, s_even, m_even)
        return 0

    last_iteration = HEAD + 8 + PAIR_LAG + HOP_LAG + TILES
    lax.fori_loop(0, (last_iteration + 1) // 2, two_iterations, 0)

    for tile in range(TILES):
        squares = ss[tile, 0:1, :]
        for d in range(3):
            pltpu.make_async_copy(sr.at[d, tile], sr.at[d, tile], s_recv.at[d, tile]).wait()
        squares = (squares + sr[0, tile, 0:1, :]) + (sr[1, tile, 0:1, :] + sr[2, tile, 0:1, :])
        o = ratio[tile] * lax.rsqrt(squares / width + 1e-06)
        out_ref[pl.ds(tile * tq, tq), :] = o.T.astype(jnp.bfloat16)

    def drained(ref, sem):
        pltpu.make_async_copy(ref, ref, send_sem.at[sem]).wait()

    drained(cs, 0)
    drained(cs_ms, 1)
    paired = pl.ds(0, VISITS - (TILES - EARLY))
    drained(ps.at[paired], 2)
    drained(ps_ms.at[paired], 3)
    drained(es, 4)
    drained(es_ms, 5)
    for b in range(1, STEPS):
        count = EARLY if b == 2 else TILES
        drained(ds.at[b - 1, pl.ds(0, count)], 2 * (2 + b))
        drained(ds_ms.at[b - 1, pl.ds(0, count)], 2 * (2 + b) + 1)
    for d in range(3):
        drained(ss, 12 + d)
    sent = qs.at[0, pl.ds(0, rows // 2)]
    for back in range(1, STEPS):
        pltpu.make_async_copy(sent, sent, q_send.at[back]).wait()
        pltpu.make_async_copy(sent, sent, f_send.at[back]).wait()


def attend(skip, start, mem_keys, mem_values, queries):
    rows, dk = queries.shape
    resident, width = mem_values.shape
    window = resident // 2
    tq = rows // TILES
    f32, bf16 = jnp.float32, jnp.bfloat16
    vmem = pltpu.VMEM
    dma = pltpu.SemaphoreType.DMA
    share = width // 4

    def both(n, dtype, *lead):
        return [vmem((n, *lead, share, tq), dtype), vmem((n, 2, tq), f32)]

    scratch = [
        pltpu.SMEM((1, 1), jnp.int32),
        pltpu.SMEM((1, 1), jnp.int32),
        vmem((resident, dk), bf16),
        vmem((resident, width), bf16),
        vmem((window, dk), bf16),
        vmem((4, share, window), bf16),
        vmem((STEPS, rows, dk), bf16),
        vmem((window, tq), f32),
        vmem((window, tq), f32),
        vmem((8, tq), f32),
        vmem((8, tq), f32),
        vmem((VISITS, 2, share, tq), f32),
        vmem((VISITS, share, tq), f32),
        *both(TILES, f32),
        vmem((TILES, share, tq), f32),
        *both(VISITS, bf16, 2),
        *both(VISITS, bf16, 2),
        *both(VISITS, bf16),
        *both(VISITS, bf16),
        *both(TILES - EARLY, bf16, 2),
        *both(TILES - EARLY, bf16, 2),
        vmem((3, TILES, share, tq), bf16),
        vmem((3, TILES, 2, tq), f32),
        vmem((3, TILES, share, tq), bf16),
        vmem((3, TILES, 2, tq), f32),
        vmem((TILES, 8, tq), f32),
        vmem((3, TILES, 8, tq), f32),
        dma((5,)),
        dma((STEPS,)), dma((STEPS, TILES)), dma((STEPS,)), dma((STEPS, TILES)),
        dma((15,)),
        dma((VISITS, 2)), dma((VISITS, 2)), dma((TILES - EARLY, 2)), dma((3, TILES, 2)),
        dma((3, TILES)),
    ]
    return pl.pallas_call(
        kernel,
        out_shape=jax.ShapeDtypeStruct((rows, share), bf16),
        in_specs=[
            pl.BlockSpec(memory_space=pl.ANY) for _ in range(5)
        ],
        out_specs=pl.BlockSpec(memory_space=vmem),
        scratch_shapes=scratch,
        compiler_params=pltpu.CompilerParams(
            collective_id=0, has_side_effects=True, vmem_limit_bytes=56 * 2**20
        ),
    )(skip, start, mem_keys, mem_values, queries)


def body(mem_keys, mem_values, offsets, block_skip, queries):
    return attend(block_skip, offsets, mem_keys, mem_values, queries)


def solution(mesh):
    placed = (
        P(("grp", "blk"), None),
        P(("grp", "blk"), None),
        P("grp", "blk"),
        P("grp", "blk"),
        P("blk", None),
    )
    return jax.shard_map(
        body, mesh=mesh, in_specs=placed, out_specs=P("blk", "grp"), check_vma=False
    )
```

```python
import jax
import jax.numpy as jnp
from jax import lax
from jax.experimental import pallas as pl
from jax.experimental.pallas import tpu as pltpu
from jax.sharding import PartitionSpec as P

MESH = pl.DeviceIdType.MESH
LOG2E = 1.4426950408889634
LOWEST = -1e30
HIGHEST = 3e38
TILES = 4
STEPS = 4
VISITS = TILES * STEPS
CHUNKS = 8
HEAD = 3
EARLY = 3
Q_LAG = 3
Q_AHEAD = 4
CORE_LAG = 1
PAIR_LAG = 4
HOP_LAG = 3


def joined(parts):
    tops = [ms[0:1, :] for _, ms in parts]
    top = tops[0]
    for other in tops[1:]:
        top = jnp.maximum(top, other)
    total = None
    sums = None
    for (values, ms), own_top in zip(parts, tops):
        f = jnp.exp2(own_top - top)
        mass = ms[1:2, :] * f
        terms = [v.astype(jnp.float32) * f for v in values]
        total = mass if total is None else total + mass
        sums = terms if sums is None else [a + b for a, b in zip(sums, terms)]
    return sums, top, total


def kernel(
    skip_hbm, start_hbm, k_hbm, v_hbm, q_hbm, out_ref,
    skip_ref, start_ref, k_all, v_all, kw, vt, qs, s_even, s_odd, m_even, m_odd,
    own, keep, home, home_ms, ratio,
    cs, cs_ms, cr, cr_ms, ps, ps_ms, pr, pr_ms,
    es, es_ms, er, er_ms, ds, ds_ms, dr, dr_ms, ss, sr,
    load_sem, q_send, q_recv, f_send, f_recv,
    send_sem, c_recv, p_recv, e_recv, d_recv, s_recv,
):
    g = lax.axis_index("grp")
    j = lax.axis_index("blk")
    nb = lax.axis_size("blk")
    core = lax.rem(g, 2)
    xl = lax.div(g, 2)
    g_core = g + 1 - 2 * core
    g_pair = lax.rem(g + 2, 4)
    g_both = g_core + 2 - 4 * xl

    def at(d):
        return lax.rem(j + nb + d, nb)

    rows = q_hbm.shape[0]
    tq = rows // TILES
    half = tq // 2
    window = kw.shape[0]
    width = v_all.shape[1]
    share = width // 4
    scale = q_hbm.shape[1] ** (-0.5) * LOG2E

    loads = [
        pltpu.make_async_copy(src, dst, load_sem.at[i])
        for i, (src, dst) in enumerate(
            ((start_hbm, start_ref), (skip_hbm, skip_ref), (q_hbm, qs.at[0]), (k_hbm, k_all), (v_hbm, v_all))
        )
    ]
    for load in loads:
        load.start()

    barrier = pltpu.get_barrier_semaphore()
    partners = [
        (g_core, j), (g_pair, j), (g_both, j), (g, at(2)), (g, at(-2)),
        (g_pair, at(1)), (g_pair, at(-1)), (g_pair, at(3)), (g_pair, at(-3)),
    ]
    for partner in partners:
        pl.semaphore_signal(barrier, inc=1, device_id=partner, device_id_type=MESH)

    def remote(src, dst, send, recv, device):
        return pltpu.make_async_remote_copy(
            src_ref=src, dst_ref=dst, send_sem=send, recv_sem=recv,
            device_id=device, device_id_type=MESH,
        )

    homes = {1: (g_pair, at(1)), 2: (g, at(2)), 3: (g_pair, at(3))}

    def q_rows(tile, part):
        return pl.ds(tile * tq + part * half, half)

    def q_copy(back, tile):
        return remote(
            qs.at[0, q_rows(tile, core)], qs.at[back, q_rows(tile, core)],
            q_send.at[back], q_recv.at[back, tile], homes[back],
        )

    def q_forward(back, tile):
        piece = qs.at[back, q_rows(tile, core)]
        pltpu.make_async_copy(piece, piece, q_recv.at[back, tile]).wait()
        remote(piece, piece, f_send.at[back], f_recv.at[back, tile], (g_core, j)).start()

    def q_wait(back, tile):
        piece = qs.at[back, q_rows(tile, 1 - core)]
        pltpu.make_async_copy(piece, piece, f_recv.at[back, tile]).wait()

    for load in loads[:3]:
        load.wait()
    pl.semaphore_wait(barrier, len(partners))
    for tile in range(Q_AHEAD):
        q_copy(2, tile).start()
    loads[3].wait()
    start = start_ref[0, 0]

    def windowed(ref, begin, size):
        low = ref[begin : begin + size, :].astype(jnp.float32)
        high = ref[window + begin : window + begin + size, :].astype(jnp.float32)
        row = begin + lax.broadcasted_iota(jnp.int32, low.shape, 0)
        return jnp.where(row >= start, low, high).astype(jnp.bfloat16)

    piece_rows = window // 8
    for c in range(8):
        kw[c * piece_rows : (c + 1) * piece_rows, :] = windowed(k_all, c * piece_rows, piece_rows)
    loads[4].wait()
    for c in range(8):
        piece = windowed(v_all, c * piece_rows, piece_rows)
        for q in range(4):
            spot = 2 * lax.rem(core + q % 2, 2) + q // 2
            vt[spot, :, c * piece_rows : (c + 1) * piece_rows] = piece[
                :, q * share : (q + 1) * share
            ].T

    def two(data_src, ms_src, data_dst, ms_dst, sem, recv, device):
        remote(data_src, data_dst, send_sem.at[2 * sem], recv.at[0], device).start()
        remote(ms_src, ms_dst, send_sem.at[2 * sem + 1], recv.at[1], device).start()

    def arrived(data, ms, recv):
        pltpu.make_async_copy(data, data, recv.at[0]).wait()
        pltpu.make_async_copy(ms, ms, recv.at[1]).wait()

    def visit(n):
        m = n - HEAD
        phase = lax.div(m + 4, 4) - 1
        remote_visit = jnp.logical_and(m >= 0, m < 12)
        back = jnp.where(phase == 2, 1, phase + 2)
        back = jnp.where(remote_visit, back, 0)
        tile = jnp.where(remote_visit, m - 4 * phase, jnp.where(m < 0, n, n - 12))
        return back, tile

    def scores(n, s_ref, c, chunk, q):
        part = slice(c * chunk, (c + 1) * chunk)
        s = lax.dot_general(
            kw[part, :], q, (((1,), (1,)), ((), ())), preferred_element_type=jnp.float32
        )
        s_ref[part, :] = s
        return jnp.max(s, axis=0, keepdims=True)

    def queries_of(n):
        back, tile = visit(n)
        return qs[back, pl.ds(pl.multiple_of(tile * tq, tq), tq), :]

    chunk = window // CHUNKS

    def compute(n, s_now, m_now, s_next, m_next):
        back, _ = visit(n)
        kept = skip_ref[0, 0] != lax.rem(j + nb - back, nb)
        q = queries_of(jnp.minimum(n + 1, VISITS - 1))
        top = m_now[0:1, :]
        ref = jnp.where(kept, top, HIGHEST)
        high = total = None
        probs = []
        for c in range(CHUNKS):
            part = slice(c * chunk, (c + 1) * chunk)
            peak = scores(n, s_next, c, chunk, q)
            high = peak if high is None else jnp.maximum(high, peak)
            p = jnp.exp2((s_now[part, :] - ref) * scale)
            mass = jnp.sum(p, axis=0, keepdims=True)
            total = mass if total is None else total + mass
            probs.append(p.astype(jnp.bfloat16))
        m_next[0:1, :] = high
        acc = jnp.dot(
            vt[...].reshape(width, window), jnp.concatenate(probs, axis=0),
            preferred_element_type=jnp.float32,
        )
        own[n, 0] = acc[0:share]
        own[n, 1] = acc[share : 2 * share]
        cs[n, 0] = acc[2 * share : 3 * share].astype(jnp.bfloat16)
        cs[n, 1] = acc[3 * share : 4 * share].astype(jnp.bfloat16)
        cs_ms[n, 0:1, :] = jnp.where(kept, top * scale, LOWEST)
        cs_ms[n, 1:2, :] = total
        two(cs.at[n], cs_ms.at[n], cr.at[n], cr_ms.at[n], 0, c_recv.at[n], (g_core, j))

    def core_merge(n):
        back, tile = visit(n)
        kx = jnp.where(lax.rem(back, 2) == 0, xl, 1 - xl)
        late = tile >= EARLY
        slot = jnp.maximum(tile - EARLY, 0)
        arrived(cr.at[n], cr_ms.at[n], c_recv.at[n])

        def chip(a, b):
            return [
                ([own[n, a], own[n, b]], cs_ms[n]),
                ([cr[n, a], cr[n, b]], cr_ms[n]),
            ]

        def to_pair(parts):
            (stay, go), top, total = joined(parts)
            keep[n] = stay
            ps[n] = go.astype(jnp.bfloat16)
            ps_ms[n, 0:1, :] = top
            ps_ms[n, 1:2, :] = total
            two(ps.at[n], ps_ms.at[n], pr.at[n], pr_ms.at[n], 1, p_recv.at[n], (g_pair, j))

        @pl.when(jnp.logical_not(jnp.logical_and(late, lax.rem(back, 2) == 0)))
        def _():
            to_pair(chip(kx, 1 - kx))

        @pl.when(jnp.logical_and(late, back == 0))
        def _():
            arrived(er.at[slot], er_ms.at[slot], e_recv.at[slot])
            more = ([er[slot, kx], er[slot, 1 - kx]], er_ms[slot])
            to_pair(chip(kx, 1 - kx) + [more])

        @pl.when(jnp.logical_and(late, back == 2))
        def _():
            (low, high), top, total = joined(chip(0, 1))
            es[slot, 0] = low.astype(jnp.bfloat16)
            es[slot, 1] = high.astype(jnp.bfloat16)
            es_ms[slot, 0:1, :] = top
            es_ms[slot, 1:2, :] = total
            two(
                es.at[slot], es_ms.at[slot], er.at[slot], er_ms.at[slot], 2, e_recv.at[slot],
                (g, at(-2)),
            )

    def pair_merge(n):
        back, tile = visit(n)

        def paired():
            arrived(pr.at[n], pr_ms.at[n], p_recv.at[n])
            (res,), top, total = joined([([keep[n]], ps_ms[n]), ([pr[n]], pr_ms[n])])
            return res, top, total

        @pl.when(back == 0)
        def _():
            res, top, total = paired()
            home[tile] = res
            home_ms[tile, 0:1, :] = top
            home_ms[tile, 1:2, :] = total

        def send_home(b):
            res, top, total = paired()
            ds[b - 1, tile] = res.astype(jnp.bfloat16)
            ds_ms[b - 1, tile, 0:1, :] = top
            ds_ms[b - 1, tile, 1:2, :] = total
            two(
                ds.at[b - 1, tile], ds_ms.at[b - 1, tile], dr.at[b - 1, tile],
                dr_ms.at[b - 1, tile], 2 + b, d_recv.at[b - 1, tile],
                (g if b == 2 else g_pair, at(-b)),
            )

        for b in (1, 3):
            @pl.when(back == b)
            def _():
                send_home(b)

        @pl.when(jnp.logical_and(back == 2, tile < EARLY))
        def _():
            send_home(2)

    def finish(tile):
        def collect(backs):
            for b in backs:
                arrived(dr.at[b - 1, tile], dr_ms.at[b - 1, tile], d_recv.at[b - 1, tile])
            (res,), _, total = joined(
                [([home[tile]], home_ms[tile])]
                + [([dr[b - 1, tile]], dr_ms[b - 1, tile]) for b in backs]
            )
            r = res / total
            ratio[tile] = r
            ss[tile] = jnp.broadcast_to(jnp.sum(r * r, axis=0, keepdims=True), ss.shape[1:])

        @pl.when(tile < EARLY)
        def _():
            collect((1, 2, 3))

        @pl.when(tile >= EARLY)
        def _():
            collect((1, 3))

        for d, partner in enumerate((g_core, g_pair, g_both)):
            remote(
                ss.at[tile], sr.at[d, tile], send_sem.at[12 + d], s_recv.at[d, tile], (partner, j)
            ).start()

    def send_visit(n):
        back, tile = visit(n)
        for b in range(1, STEPS):
            @pl.when(back == b)
            def _():
                q_copy(b, tile).start()

    def forward_visit(n):
        back, tile = visit(n)
        for b in range(1, STEPS):
            @pl.when(back == b)
            def _():
                q_forward(b, tile)

    def wait_visit(n):
        back, tile = visit(n)

        @pl.when(back > 0)
        def _():
            q_wait(back, tile)

    def iteration(n, s_now, m_now, s_next, m_next):
        @pl.when(n < 12 - Q_AHEAD)
        def _():
            send_visit(n + HEAD + Q_AHEAD)

        @pl.when(n < VISITS - 1)
        def _():
            wait_visit(n + 1)

        @pl.when(n < VISITS)
        def _():
            compute(n, s_now, m_now, s_next, m_next)

        @pl.when(n == 0)
        def _():
            core_merge(n)

        @pl.when(jnp.logical_and(n >= CORE_LAG + 1, n < VISITS + CORE_LAG))
        def _():
            core_merge(n - CORE_LAG)

        @pl.when(jnp.logical_and(n >= PAIR_LAG, n < VISITS + PAIR_LAG))
        def _():
            pair_merge(n - PAIR_LAG)

        @pl.when(n < VISITS - Q_LAG)
        def _():
            forward_visit(n + Q_LAG)

        last = HEAD + 8 + PAIR_LAG + HOP_LAG

        @pl.when(jnp.logical_and(n >= last, n < last + TILES))
        def _():
            finish(n - last)

    q0 = queries_of(0)
    high = None
    for c in range(CHUNKS):
        peak = scores(0, s_even, c, chunk, q0)
        high = peak if high is None else jnp.maximum(high, peak)
    m_even[0:1, :] = high

    def two_iterations(u, _):
        iteration(2 * u, s_even, m_even, s_odd, m_odd)
        iteration(2 * u + 1, s_odd, m_odd, s_even, m_even)
        return 0

    last_iteration = HEAD + 8 + PAIR_LAG + HOP_LAG + TILES
    lax.fori_loop(0, (last_iteration + 1) // 2, two_iterations, 0)

    for tile in range(TILES):
        squares = ss[tile, 0:1, :]
        for d in range(3):
            pltpu.make_async_copy(sr.at[d, tile], sr.at[d, tile], s_recv.at[d, tile]).wait()
        squares = (squares + sr[0, tile, 0:1, :]) + (sr[1, tile, 0:1, :] + sr[2, tile, 0:1, :])
        o = ratio[tile] * lax.rsqrt(squares / width + 1e-06)
        out_ref[pl.ds(tile * tq, tq), :] = o.T.astype(jnp.bfloat16)

    def drained(ref, sem):
        pltpu.make_async_copy(ref, ref, send_sem.at[sem]).wait()

    drained(cs, 0)
    drained(cs_ms, 1)
    paired = pl.ds(0, VISITS - (TILES - EARLY))
    drained(ps.at[paired], 2)
    drained(ps_ms.at[paired], 3)
    drained(es, 4)
    drained(es_ms, 5)
    for b in range(1, STEPS):
        count = EARLY if b == 2 else TILES
        drained(ds.at[b - 1, pl.ds(0, count)], 2 * (2 + b))
        drained(ds_ms.at[b - 1, pl.ds(0, count)], 2 * (2 + b) + 1)
    for d in range(3):
        drained(ss, 12 + d)
    sent = qs.at[0, pl.ds(0, rows // 2)]
    for back in range(1, STEPS):
        pltpu.make_async_copy(sent, sent, q_send.at[back]).wait()
        pltpu.make_async_copy(sent, sent, f_send.at[back]).wait()


def attend(skip, start, mem_keys, mem_values, queries):
    rows, dk = queries.shape
    resident, width = mem_values.shape
    window = resident // 2
    tq = rows // TILES
    f32, bf16 = jnp.float32, jnp.bfloat16
    vmem = pltpu.VMEM
    dma = pltpu.SemaphoreType.DMA
    share = width // 4

    def both(n, dtype, *lead):
        return [vmem((n, *lead, share, tq), dtype), vmem((n, 2, tq), f32)]

    scratch = [
        pltpu.SMEM((1, 1), jnp.int32),
        pltpu.SMEM((1, 1), jnp.int32),
        vmem((resident, dk), bf16),
        vmem((resident, width), bf16),
        vmem((window, dk), bf16),
        vmem((4, share, window), bf16),
        vmem((STEPS, rows, dk), bf16),
        vmem((window, tq), f32),
        vmem((window, tq), f32),
        vmem((8, tq), f32),
        vmem((8, tq), f32),
        vmem((VISITS, 2, share, tq), f32),
        vmem((VISITS, share, tq), f32),
        *both(TILES, f32),
        vmem((TILES, share, tq), f32),
        *both(VISITS, bf16, 2),
        *both(VISITS, bf16, 2),
        *both(VISITS, bf16),
        *both(VISITS, bf16),
        *both(TILES - EARLY, bf16, 2),
        *both(TILES - EARLY, bf16, 2),
        vmem((3, TILES, share, tq), bf16),
        vmem((3, TILES, 2, tq), f32),
        vmem((3, TILES, share, tq), bf16),
        vmem((3, TILES, 2, tq), f32),
        vmem((TILES, 8, tq), f32),
        vmem((3, TILES, 8, tq), f32),
        dma((5,)),
        dma((STEPS,)), dma((STEPS, TILES)), dma((STEPS,)), dma((STEPS, TILES)),
        dma((15,)),
        dma((VISITS, 2)), dma((VISITS, 2)), dma((TILES - EARLY, 2)), dma((3, TILES, 2)),
        dma((3, TILES)),
    ]
    return pl.pallas_call(
        kernel,
        out_shape=jax.ShapeDtypeStruct((rows, share), bf16),
        in_specs=[
            pl.BlockSpec(memory_space=pl.ANY) for _ in range(5)
        ],
        out_specs=pl.BlockSpec(memory_space=vmem),
        scratch_shapes=scratch,
        compiler_params=pltpu.CompilerParams(
            collective_id=0, has_side_effects=True, vmem_limit_bytes=56 * 2**20
        ),
    )(skip, start, mem_keys, mem_values, queries)


def body(mem_keys, mem_values, offsets, block_skip, queries):
    return attend(block_skip, offsets, mem_keys, mem_values, queries)


def solution(mesh):
    placed = (
        P(("grp", "blk"), None),
        P(("grp", "blk"), None),
        P("grp", "blk"),
        P("grp", "blk"),
        P("blk", None),
    )
    return jax.shard_map(
        body, mesh=mesh, in_specs=placed, out_specs=P("blk", "grp"), check_vma=False
    )
```
